32 devices in a mesh: dp: 8 (over z, core), shard: 4 (over y, x).
Axes of the slice: x: 2, y: 2, z: 4, core: 2. Of those that a mesh axis runs over, the one named last changes fastest.
Arguments:
- momentum: bfloat16 [8, 2, 4096, 1536], P('dp', None, 'shard'), may hold values from -6 to 6
- right_basis: bfloat16 [8, 2, 128, 1536], P('dp'), as said below
- reach_map: int32 [8, 64], replicated, may hold values from 0 to 1, as said below
Outputs:
- momentum_next: bfloat16 [8, 2, 4096, 1536], P('dp', None, 'shard')
- basis_next: bfloat16 [8, 2, 128, 1536], P('dp')
- left_factor: bfloat16 [8, 2, 4096, 128], P('dp', None, 'shard')
The draws below stay inside these ranges and needn't reach their ends.
Inputs may be any that keep to these rules, and one draw needn't show every extreme that they name: `reach_map`: each row holds exactly 2 ones; the ones of a row lie in different blocks of 16 consecutive experts; in every draw one block holds a one of every row. Slots of any replicas that hold the same expert hold equal right_basis.
All inputs are finite; a program needn't handle non-finite values.
Results may differ from the reference program's by a relative error of at most 0.018.
Values may be sent and summed in bfloat16 or wider, within the bound.
A program may use at most 64 MiB of HBM per device.

```python
import math
import jax
import jax.numpy as jnp
from jax import lax

ROWS = 4096
COLS = 1536
RANK = 128
EXPERTS = 64
NGROUP = 4
SLOTS = 2
REPLICAS = 8
EXP_GRP = 16
N_SHARD = 4


def reach_pattern(key):
    hot_block = jax.random.randint(jax.random.fold_in(key, 41), (), 0, NGROUP)
    row_keys = jax.random.split(jax.random.fold_in(key, 44), REPLICAS)
    orders = jax.vmap(lambda k: jax.random.permutation(k, NGROUP - 1))(row_keys).astype(jnp.int32)
    others = orders[:, :SLOTS - 1]
    others = others + (others >= hot_block).astype(jnp.int32)
    hot_column = jnp.zeros((REPLICAS, 1), jnp.int32) + hot_block
    blocks = jnp.concatenate([hot_column, others], axis=1)
    picks = jax.random.randint(jax.random.fold_in(key, 42), (REPLICAS, SLOTS), 0, EXP_GRP)
    chosen_ids = blocks * EXP_GRP + picks
    expert_ids = jnp.arange(EXPERTS, dtype=jnp.int32)
    pattern = jnp.sum((expert_ids[None, None, :] == chosen_ids[:, :, None]).astype(jnp.int32), axis=1)
    return pattern.astype(jnp.int32)


def draw_reach_map(key, part):
    return reach_pattern(key)


def draw_right_basis(key, part):
    pattern = reach_pattern(key)
    key = jax.random.fold_in(key, 5)
    table = jax.random.normal(key, (EXPERTS, RANK, COLS), jnp.float32)
    counts = jnp.cumsum(pattern, axis=1)
    expert_ids = jnp.arange(EXPERTS, dtype=jnp.int32)
    slot_ids = jnp.stack([jnp.sum(((pattern == 1) & (counts == k + 1)).astype(jnp.int32) * expert_ids[None, :], axis=1) for k in range(SLOTS)], axis=1)
    return table[slot_ids].astype(jnp.bfloat16)


def block_levels(key, extent, shards, low, largest):
    def one(axis_at, shards_of):
        steps = jax.random.uniform(jax.random.fold_in(jax.random.fold_in(key, 6), axis_at), (shards_of,), jnp.float32, low / len(shards), largest / len(shards))
        return jnp.repeat(jnp.exp(steps), extent[axis_at] // shards_of).reshape((-1,) + (1,) * (len(extent) - axis_at - 1))

    factor_of = one(*shards[0])
    for cut in shards[1:]:
        factor_of = factor_of * one(*cut)
    return factor_of


def scatter_about(stream_key, extent, width, reach, cuts=(), kind=jnp.bfloat16):
    values = jax.random.normal(stream_key, extent, jnp.float32) * width
    if len(cuts) > 0:
        values = block_levels(stream_key, extent, cuts, -0.22, 0.18) * values
    return jnp.clip(values, min=-reach, max=reach).astype(kind)


def setup_inputs(seed: int = 0) -> dict:
    key_of = jax.random.split(jax.random.key(seed), 4)
    momentum = scatter_about(key_of[0], (REPLICAS, SLOTS, ROWS, COLS), 1.0, 6.0, ((0, 8), (2, 4)))
    right_basis = draw_right_basis(jax.random.fold_in(key_of[3], 71), 0)
    reach_map = draw_reach_map(jax.random.fold_in(key_of[3], 71), 0)
    return dict(momentum=momentum, right_basis=right_basis, reach_map=reach_map)


decay_keep = 0.9

def reference(momentum, right_basis, reach_map):
    counts = jnp.cumsum(reach_map, axis=1)
    chosen = jnp.stack([((reach_map == 1) & (counts == k + 1)).astype(jnp.int32) for k in range(SLOTS)], axis=1)
    expert_ids = lax.broadcasted_iota(jnp.int32, (EXPERTS,), 0)
    slot_expert = lax.optimization_barrier(jnp.sum(chosen * expert_ids[None, None, :], axis=2)).astype(jnp.int32)

    def one_partial(items):
        block_data, basis_data = items
        product = jnp.einsum('src,skc->srk', block_data.astype(jnp.float32), basis_data.astype(jnp.float32))
        return (product * (1.0 / math.sqrt(COLS))).astype(jnp.bfloat16)
    partials = lax.map(one_partial, (momentum, right_basis))
    left_sum = jnp.zeros((EXPERTS, ROWS, RANK), jnp.float32)
    left_sum = left_sum.at[slot_expert.reshape(-1)].add(partials.reshape(-1, ROWS, RANK).astype(jnp.float32))
    reach_count = lax.optimization_barrier(jnp.sum(reach_map, axis=0))
    identity = jnp.eye(RANK, dtype=jnp.float32)
    gram_sum = jnp.einsum('exa,exb->eab', left_sum, left_sum, precision=lax.Precision.HIGHEST)
    gram_sum = gram_sum + identity[None] * (reach_count == 0).astype(jnp.float32)[:, None, None]
    factor = jnp.linalg.cholesky(gram_sum)
    inverse = jax.vmap(lambda m: jax.scipy.linalg.solve_triangular(m, identity, lower=True))(factor)
    scaled = inverse * math.sqrt(ROWS)
    ortho_rows = jnp.einsum('exk,eyk->exy', left_sum, scaled, precision=lax.Precision.HIGHEST).astype(jnp.bfloat16)
    left_factor = ortho_rows[slot_expert]

    def one_update(items):
        block_data, left_data = items
        block_wide = block_data.astype(jnp.float32)
        left_wide = left_data.astype(jnp.float32)
        block_split = block_wide.reshape(SLOTS, N_SHARD, ROWS // N_SHARD, COLS)
        left_split = left_wide.reshape(SLOTS, N_SHARD, ROWS // N_SHARD, RANK)
        right_part = jnp.einsum('snxk,snxc->snkc', left_split, block_split) * (1.0 / math.sqrt(ROWS))
        right_part = lax.optimization_barrier(right_part.astype(jnp.bfloat16)).astype(jnp.float32)
        right_full = lax.optimization_barrier(jnp.sum(right_part, axis=1)).astype(jnp.bfloat16)
        right_wide = right_full.astype(jnp.float32)
        basis_next = (right_wide * lax.rsqrt(lax.optimization_barrier(jnp.mean(right_wide * right_wide, axis=2, keepdims=True)) + 1e-06)).astype(jnp.bfloat16)
        update = jnp.einsum('sxk,skc->sxc', left_wide, right_wide)
        momentum_next = (block_wide - (1.0 - decay_keep) / math.sqrt(ROWS) * update).astype(jnp.bfloat16)
        return (momentum_next, basis_next)
    momentum_next, basis_next = lax.map(one_update, (momentum, left_factor))
    return (momentum_next, basis_next, left_factor)
```

```python
import functools
import math

import jax
import jax.numpy as jnp
from jax import lax
from jax.experimental import pallas as pl
from jax.experimental.pallas import tpu as pltpu
from jax.sharding import PartitionSpec as P

NGROUP = 4


decay_keep = 0.9


def from_partner(value, axis, stride):
    mask = 2**stride
    pairs = [(source, source ^ mask) for source in range(lax.axis_size(axis))]
    return lax.ppermute(value, axis, pairs)


def slot_table(reach_map, slot_count):
    counts = jnp.cumsum(reach_map, axis=1)
    chosen = [((reach_map == 1) & (counts == k + 1)).astype(jnp.int32) for k in range(slot_count)]
    return jnp.stack(chosen, axis=1)


def on_device(momentum, right_basis, reach_map):
    slot_count = momentum.shape[1]
    rows_dev = momentum.shape[2]
    col_count = momentum.shape[3]
    rank_size = right_basis.shape[2]
    experts = reach_map.shape[1]
    groups = NGROUP
    replicas = lax.axis_size("dp")
    group_size = replicas // groups
    rows_own = rows_dev // group_size
    per_group = experts // groups
    per_shard = per_group // lax.axis_size("shard")
    shard_pos = lax.axis_index("shard")
    device = lax.axis_index("dp")
    owner_group = device // group_size
    total_rows = rows_dev * lax.axis_size("shard")
    slot_hits = slot_table(reach_map, slot_count)
    expert_group = lax.broadcasted_iota(jnp.int32, (experts,), 0) // per_group
    group_ids = lax.broadcasted_iota(jnp.int32, (groups,), 0)
    my_slots = lax.dynamic_index_in_dim(slot_hits, device, 0, keepdims=False)
    slot_group = jnp.sum(my_slots * expert_group[None, :], axis=1)
    slot_onehot = (slot_group[:, None] == group_ids[None, :]).astype(jnp.bfloat16)
    partial_value = jnp.einsum(
        "src,skc->srk", momentum[0], right_basis[0], preferred_element_type=jnp.float32
    )
    partial_value = (partial_value * (1.0 / math.sqrt(col_count))).astype(jnp.bfloat16)
    pieces = partial_value.reshape(slot_count, group_size, rows_own, rank_size)
    outgoing = jnp.einsum(
        "sg,sqxk->gqxk", slot_onehot, pieces, preferred_element_type=jnp.float32
    ).astype(jnp.bfloat16)
    outgoing = outgoing.reshape(replicas, rows_own, rank_size)
    incoming = lax.all_to_all(outgoing, "dp", split_axis=0, concat_axis=0, tiled=True)
    owned_hits = lax.dynamic_slice_in_dim(slot_hits, owner_group * per_group, per_group, 2)
    source_owned = jnp.sum(owned_hits, axis=1)
    own_count = jnp.sum(source_owned, axis=0)
    my_count = lax.dynamic_slice_in_dim(own_count, shard_pos * per_shard, per_shard, 0)
    source_weight = source_owned.astype(jnp.bfloat16)
    left_sum = jnp.einsum(
        "rj,rxk->jxk", source_weight, incoming, preferred_element_type=jnp.float32
    )
    gram_local = jnp.einsum("jxa,jxb->jab", left_sum, left_sum, precision=lax.Precision.HIGHEST)
    bit_count = group_size.bit_length() - 1
    gram_sum = lax.psum(gram_local.astype(jnp.bfloat16), "shard").astype(jnp.float32)
    for level in range(bit_count):
        gram_sum = gram_sum + from_partner(gram_sum.astype(jnp.bfloat16), "dp", level).astype(
            gram_sum.dtype
        )
    my_gram = lax.dynamic_slice_in_dim(gram_sum, shard_pos * per_shard, per_shard, 0)
    identity = jnp.eye(rank_size, dtype=jnp.float32)
    my_gram = my_gram + identity[None] * (my_count == 0).astype(jnp.float32)[:, None, None]
    factor = jnp.linalg.cholesky(my_gram)
    my_inverse = jax.vmap(lambda m: jax.scipy.linalg.solve_triangular(m, identity, lower=True))(
        factor
    )
    inverse = lax.all_gather(my_inverse.astype(jnp.bfloat16), "shard", axis=0, tiled=True).astype(
        my_inverse.dtype
    )
    scaled = inverse * math.sqrt(total_rows)
    ortho_rows = jnp.einsum(
        "jxk,jyk->jxy", left_sum, scaled, precision=lax.Precision.HIGHEST
    ).astype(jnp.bfloat16)
    send_back = jnp.einsum(
        "rj,jxy->rxy", source_weight, ortho_rows, preferred_element_type=jnp.float32
    ).astype(jnp.bfloat16)
    arrived = lax.all_to_all(send_back, "dp", split_axis=0, concat_axis=0, tiled=True)
    arrived = arrived.reshape(groups, group_size, rows_own, rank_size)
    left_factor = jnp.einsum(
        "sg,gqxk->sqxk", slot_onehot, arrived, preferred_element_type=jnp.float32
    ).astype(jnp.bfloat16)
    left_factor = left_factor.reshape(slot_count, rows_dev, rank_size)
    right_part = jnp.einsum(
        "srk,src->skc", left_factor, momentum[0], preferred_element_type=jnp.float32
    )
    right_part = (right_part * (1.0 / math.sqrt(total_rows))).astype(jnp.bfloat16)
    right_share = (
        lax.psum_scatter(right_part, "shard", scatter_dimension=1, tiled=True)
        .astype(jnp.float32)
        .astype(jnp.bfloat16)
    )
    right_full = lax.all_gather(right_share, "shard", axis=1, tiled=True)
    right_wide = right_full.astype(jnp.float32)
    basis_next = (
        right_wide * lax.rsqrt(jnp.mean(right_wide * right_wide, axis=2, keepdims=True) + 1e-06)
    ).astype(jnp.bfloat16)
    update = jnp.einsum("sxk,skc->sxc", left_factor, right_full, preferred_element_type=jnp.float32)
    momentum_next = (
        momentum[0].astype(jnp.float32) - (1.0 - decay_keep) / math.sqrt(total_rows) * update
    ).astype(jnp.bfloat16)
    return (momentum_next[None], basis_next[None], left_factor[None])


MESH = pl.DeviceIdType.MESH
ROUND = 8
EARLY_ROUNDS = 5


def remote(src, dst, send_sem, recv_sem, device):
    return pltpu.make_async_remote_copy(
        src_ref=src,
        dst_ref=dst,
        send_sem=send_sem,
        recv_sem=recv_sem,
        device_id=device,
        device_id_type=MESH,
    )


def dot_nt(a, b):
    return lax.dot_general(a, b, (((1,), (1,)), ((), ())), preferred_element_type=jnp.float32)


def dot_tn(a, b):
    return lax.dot_general(a, b, (((0,), (0,)), ((), ())), preferred_element_type=jnp.float32)


def slot_classes(reach, groups):
    lane = lax.broadcasted_iota(jnp.int32, reach.shape, 1)
    width = reach.shape[1] // groups
    hot_lanes = jnp.zeros(reach.shape, jnp.float32)
    taken = jnp.zeros((1, 1), jnp.float32)
    for group in range(groups):
        inside = ((lane >= group * width) & (lane < (group + 1) * width)).astype(jnp.float32)
        row_count = jnp.sum(reach * inside, axis=1, keepdims=True)
        full = jnp.min(row_count, axis=0, keepdims=True)
        pick = jnp.where(full > 0.5, 1.0, 0.0) * (1.0 - taken)
        taken = taken + pick
        hot_lanes = hot_lanes + pick * inside
    lane_id = lane.astype(jnp.float32)
    hot = jnp.sum(reach * hot_lanes * lane_id, axis=1, keepdims=True)
    cold = jnp.sum(reach * (1.0 - hot_lanes) * lane_id, axis=1, keepdims=True)
    return hot, cold


def eliminate_round(step, mat):
    rank = mat.shape[1]
    row_id = lax.broadcasted_iota(jnp.int32, mat.shape, 1)
    lane_id = lax.broadcasted_iota(jnp.int32, mat.shape, 2)
    left = rank - ROUND * step
    for m in range(ROUND):
        row = mat[:, m : m + 1, :]
        pivot = 1.0 / row[:, :, m : m + 1]
        active = (row_id > m) & (row_id < left)
        ratio = jnp.where(active, mat[:, :, m : m + 1] * pivot, 0.0)
        row_one = jnp.where(lane_id[:, :1] == m, 1.0, row)
        mat = jnp.where(active & (lane_id == m), 0.0, mat) - ratio * row_one
    mat = jnp.concatenate([mat[:, ROUND:], mat[:, :ROUND]], axis=1)
    return pltpu.roll(mat, rank - ROUND, axis=2)


def power_kernel(
    groups,
    m_hbm,
    b_hbm,
    reach_ref,
    q_ref,
    inv_ref,
    r_ref,
    m_buf,
    b_buf,
    p_out,
    p_in,
    q_out,
    q_in,
    g_out,
    g_in,
    x_out,
    x_in,
    t_out,
    t_in,
    t_red,
    t_full,
    m_sem,
    b_sem,
    p_send,
    p_recv,
    q_send,
    q_recv,
    g_send,
    g_recv,
    x_send,
    x_recv,
    t_send,
    t_recv,
    f_send,
    f_recv,
):
    me = lax.axis_index("dp")
    sp = lax.axis_index("shard")
    replicas = p_in.shape[0]
    pieces = replicas // 2
    rows = p_in.shape[1]
    shards = t_full.shape[0]
    wide = t_full.shape[3]
    cols = m_buf.shape[2]
    rank = b_buf.shape[1]
    core = lax.rem(me, 2)
    zed = me // 2
    order = list(range(pieces // 2, pieces)) + list(range(1, pieces // 2)) + [0]

    def piece_at(o):
        return lax.rem(zed + o, pieces)

    def span(q):
        return pl.ds(pl.multiple_of(q * rows, rows), rows)

    for k in range(2):
        pltpu.make_async_copy(b_hbm.at[k], b_buf.at[k], b_sem.at[k]).start()
    for o in order:
        for k in range(2):
            at = span(piece_at(o))
            pltpu.make_async_copy(m_hbm.at[k, at], m_buf.at[k, at], m_sem.at[o, k]).start()

    barrier = pltpu.get_barrier_semaphore()
    for o in range(1, replicas):
        pl.semaphore_signal(barrier, 1, device_id=(lax.rem(me + o, replicas), sp), device_id_type=MESH)
    for o in range(1, shards):
        for cc in range(2):
            pl.semaphore_signal(
                barrier, 1, device_id=(2 * zed + cc, lax.rem(sp + o, shards)), device_id_type=MESH
            )

    hot, cold = slot_classes(reach_ref[...].astype(jnp.float32), groups)
    mine = lax.broadcasted_iota(jnp.int32, (replicas, 1), 0) == me
    my_hot = jnp.sum(jnp.where(mine, hot, 0.0), axis=0, keepdims=True)
    my_cold = jnp.sum(jnp.where(mine, cold, 0.0), axis=0, keepdims=True)
    first = jnp.where(my_hot < my_cold, 1.0, 0.0)
    ids = jnp.where(core == 0, hot, cold)
    diag = lax.broadcasted_iota(jnp.int32, (replicas, replicas), 0) == lax.broadcasted_iota(
        jnp.int32, (replicas, replicas), 1
    )
    ids_row = jnp.sum(jnp.where(diag, ids, 0.0), axis=0, keepdims=True)
    same = jnp.where(ids == ids_row, 1.0, 0.0)

    for k in range(2):
        pltpu.make_async_copy(b_hbm.at[k], b_buf.at[k], b_sem.at[k]).wait()

    for n, o in enumerate(order):
        q = piece_at(o)
        at = span(q)
        part = []
        for k in range(2):
            pltpu.make_async_copy(m_hbm.at[k, at], m_buf.at[k, at], m_sem.at[o, k]).wait()
            value = dot_nt(m_buf[k, at, :], b_buf[k]) * (1.0 / math.sqrt(cols))
            part.append(value)
        p_out[o, 0] = (part[0] * first + part[1] * (1.0 - first)).astype(jnp.bfloat16)
        p_out[o, 1] = (part[1] * first + part[0] * (1.0 - first)).astype(jnp.bfloat16)
        if n == 0:
            pl.semaphore_wait(barrier, replicas - 1 + 2 * (shards - 1))
        if o > 0:
            for cc in range(2):
                remote(
                    p_out.at[o, cc], p_in.at[me], p_send.at[o, cc], p_recv.at[me], (2 * q + cc, sp)
                ).start()
        else:
            other = 1 - core
            remote(
                p_out.at[0, other], p_in.at[me], p_send.at[0, 0], p_recv.at[me], (2 * q + other, sp)
            ).start()
            p_in[me] = p_out[0, core]

    for o in range(1, replicas):
        src = lax.rem(me + o, replicas)
        remote(p_out.at[0, 0], p_in.at[src], p_send.at[0, 0], p_recv.at[src], (src, sp)).wait_recv()

    for zz in range(pieces):
        for cc in range(2):
            i = 2 * zz + cc
            total = jnp.zeros((rows, rank), jnp.float32)
            for j in range(replicas):
                total = total + same[i : i + 1, j : j + 1] * p_in[j].astype(jnp.float32)
            rounded = total.astype(jnp.bfloat16)
            q_out[i] = rounded
            g_out[zz, cc] = dot_tn(rounded, rounded).astype(jnp.bfloat16)

        @pl.when(zz != zed)
        def _():
            remote(
                g_out.at[zz], g_in.at[zed], g_send.at[zz], g_recv.at[zed], (2 * zz + core, sp)
            ).start()

        @pl.when(zz == zed)
        def _():
            g_in[zz] = g_out[zz]

    for o in range(1, replicas):
        dst = lax.rem(me + o, replicas)
        remote(
            q_out.at[dst],
            q_in.at[core, span(zed)],
            q_send.at[o],
            q_recv.at[core, zed],
            (dst, sp),
        ).start()
    q_in[core, span(zed), :] = q_out[me]

    for o in range(1, pieces):
        src = piece_at(o)
        remote(
            g_out.at[0], g_in.at[src], g_send.at[0], g_recv.at[src], (2 * src + core, sp)
        ).wait_recv()
    for cc in range(2):
        gram = g_in[0, cc].astype(jnp.float32)
        for zz in range(1, pieces):
            gram = gram + g_in[zz, cc].astype(jnp.float32)
        x_out[cc] = gram.astype(jnp.bfloat16)
    peers = [(dc, o) for o in range(shards) for dc in range(2) if (dc, o) != (0, 0)]
    for dc, o in peers:
        cc = lax.rem(core + dc, 2)
        sq = lax.rem(sp + o, shards)
        remote(
            x_out.at[cc], x_in.at[core, sp], x_send.at[dc, o], x_recv.at[core, sp], (2 * zed + cc, sq)
        ).start()
    x_in[core, sp] = x_out[core]
    for dc, o in peers:
        cc = lax.rem(core + dc, 2)
        sq = lax.rem(sp + o, shards)
        remote(
            x_out.at[0], x_in.at[cc, sq], x_send.at[dc, o], x_recv.at[cc, sq], (2 * zed + cc, sq)
        ).wait_recv()

    square = (rank, rank)
    eye_mask = lax.broadcasted_iota(jnp.int32, square, 0) == lax.broadcasted_iota(
        jnp.int32, square, 1
    )
    identity = jnp.where(eye_mask, 1.0, 0.0)
    grams = []
    for c, (table, own) in enumerate(((hot, my_hot), (cold, my_cold))):
        count = jnp.sum(jnp.where(table == own, 1.0, 0.0), axis=0, keepdims=True)
        gram = x_in[c, 0].astype(jnp.float32)
        for sq in range(1, shards):
            gram = gram + x_in[c, sq].astype(jnp.float32)
        grams.append(gram + identity * jnp.where(count < 0.5, 1.0, 0.0))
    mat = jnp.stack(grams, axis=0)
    rounds = rank // ROUND
    mat = lax.fori_loop(0, EARLY_ROUNDS, eliminate_round, mat)

    for cc in range(2):
        for zz in range(pieces):

            @pl.when((cc != core) | (zz != zed))
            def _():
                remote(
                    q_out.at[0],
                    q_in.at[cc, pl.ds(zz * rows, rows)],
                    q_send.at[0],
                    q_recv.at[cc, zz],
                    (2 * zz + cc, sp),
                ).wait_recv()

    for zz in range(pieces):
        at = pl.ds(zz * rows, rows)
        a = q_in[0, at, :].astype(jnp.float32)
        b = q_in[1, at, :].astype(jnp.float32)
        q_ref[0, at, :] = (a * first + b * (1.0 - first)).astype(jnp.bfloat16)
        q_ref[1, at, :] = (b * first + a * (1.0 - first)).astype(jnp.bfloat16)
    turned = [q_ref[k].T for k in range(2)]
    for o in list(range(1, shards)) + [0]:
        sq = lax.rem(sp + o, shards)
        at = pl.ds(pl.multiple_of(sq * wide, wide), wide)
        for k in range(2):
            value = jnp.dot(turned[k], m_buf[k, :, at], preferred_element_type=jnp.float32)
            t_out[o, k] = value.astype(jnp.bfloat16)
        if o > 0:
            remote(t_out.at[o], t_in.at[sp], t_send.at[o], t_recv.at[sp], (me, sq)).start()
        else:
            t_in[sp] = t_out[0]

    mat = lax.fori_loop(EARLY_ROUNDS, rounds, eliminate_round, mat)

    for o in range(1, shards):
        sq = lax.rem(sp + o, shards)
        remote(t_out.at[0], t_in.at[sq], t_send.at[0], t_recv.at[sq], (me, sq)).wait_recv()
    for k in range(2):
        value = t_in[0, k].astype(jnp.float32)
        for sq in range(1, shards):
            value = value + t_in[sq, k].astype(jnp.float32)
        t_red[k] = value.astype(jnp.bfloat16)
    for o in range(1, shards):
        sq = lax.rem(sp + o, shards)
        remote(t_red, t_full.at[sp], f_send.at[o], f_recv.at[sp], (me, sq)).start()
    t_full[sp] = t_red[...]

    below = lax.broadcasted_iota(jnp.int32, square, 0) > lax.broadcasted_iota(jnp.int32, square, 1)
    inverse = []
    for c in range(2):
        pivots = jnp.sum(jnp.where(eye_mask, mat[c], 0.0), axis=1, keepdims=True)
        unit = jnp.where(below, mat[c], identity)
        inverse.append(unit * lax.rsqrt(pivots))
    ordered = [
        (inverse[0] * first + inverse[1] * (1.0 - first)).astype(jnp.bfloat16),
        (inverse[1] * first + inverse[0] * (1.0 - first)).astype(jnp.bfloat16),
    ]
    for k in range(2):
        inv_ref[k] = ordered[k]

    for o in range(1, shards):
        sq = lax.rem(sp + o, shards)
        remote(t_red, t_full.at[sq], f_send.at[o], f_recv.at[sq], (me, sq)).wait_recv()
    for sq in range(shards):
        for k in range(2):
            value = jnp.dot(ordered[k], t_full[sq, k], preferred_element_type=jnp.float32)
            r_ref[k, :, sq * wide : (sq + 1) * wide] = value.astype(jnp.bfloat16)

    for o in order:
        for cc in range(2 if o > 0 else 1):
            remote(
                p_out.at[o, cc], p_in.at[me], p_send.at[o, cc], p_recv.at[me], (2 * zed + 1 - core, sp)
            ).wait_send()
    for o in range(1, replicas):
        dst = lax.rem(me + o, replicas)
        remote(
            q_out.at[dst], q_in.at[core, span(zed)], q_send.at[o], q_recv.at[core, zed], (dst, sp)
        ).wait_send()
    for zz in range(pieces):

        @pl.when(zz != zed)
        def _():
            remote(
                g_out.at[zz], g_in.at[zed], g_send.at[zz], g_recv.at[zed], (2 * zz + core, sp)
            ).wait_send()

    for dc, o in peers:
        cc = lax.rem(core + dc, 2)
        sq = lax.rem(sp + o, shards)
        remote(
            x_out.at[cc], x_in.at[core, sp], x_send.at[dc, o], x_recv.at[core, sp], (2 * zed + cc, sq)
        ).wait_send()
    for o in range(1, shards):
        sq = lax.rem(sp + o, shards)
        remote(t_out.at[o], t_in.at[sp], t_send.at[o], t_recv.at[sp], (me, sq)).wait_send()
        remote(t_red, t_full.at[sp], f_send.at[o], f_recv.at[sp], (me, sq)).wait_send()


def finish_kernel(total_rows, m_ref, q_ref, inv_ref, r_ref, out_ref, basis_ref, left_ref):
    r_value = r_ref[0]
    scale = math.sqrt(total_rows)
    left = (dot_nt(q_ref[0], inv_ref[0]) * scale).astype(jnp.bfloat16)
    left_ref[0] = left
    update = jnp.dot(left, r_value, preferred_element_type=jnp.float32)
    out_ref[0] = (m_ref[0].astype(jnp.float32) - ((1.0 - decay_keep) / scale) * update).astype(
        jnp.bfloat16
    )

    @pl.when(pl.program_id(1) == 0)
    def _():
        r_wide = r_value.astype(jnp.float32)
        mean = jnp.mean(r_wide * r_wide, axis=1, keepdims=True)
        basis_ref[0] = (r_wide * lax.rsqrt(mean + 1e-06)).astype(jnp.bfloat16)


def fused_on_device(momentum, right_basis, reach_map):
    momentum = momentum[0]
    right_basis = right_basis[0]
    slots, rows_dev, cols = momentum.shape
    rank = right_basis.shape[1]
    replicas = lax.axis_size("dp")
    shards = lax.axis_size("shard")
    pieces = replicas // 2
    rows = rows_dev // pieces
    wide = cols // shards
    bf16 = jnp.bfloat16
    dma = pltpu.SemaphoreType.DMA
    vmem = pl.BlockSpec(memory_space=pltpu.VMEM)
    hbm = pl.BlockSpec(memory_space=pl.ANY)
    q, inv, r = pl.pallas_call(
        functools.partial(power_kernel, NGROUP),
        out_shape=(
            jax.ShapeDtypeStruct((2, rows_dev, rank), bf16),
            jax.ShapeDtypeStruct((2, rank, rank), bf16),
            jax.ShapeDtypeStruct((2, rank, cols), bf16),
        ),
        in_specs=[hbm, hbm, vmem],
        out_specs=(vmem, vmem, vmem),
        scratch_shapes=[
            pltpu.VMEM((2, rows_dev, cols), bf16),
            pltpu.VMEM((2, rank, cols), bf16),
            pltpu.VMEM((pieces, 2, rows, rank), bf16),
            pltpu.VMEM((replicas, rows, rank), bf16),
            pltpu.VMEM((replicas, rows, rank), bf16),
            pltpu.VMEM((2, rows_dev, rank), bf16),
            pltpu.VMEM((pieces, 2, rank, rank), bf16),
            pltpu.VMEM((pieces, 2, rank, rank), bf16),
            pltpu.VMEM((2, rank, rank), bf16),
            pltpu.VMEM((2, shards, rank, rank), bf16),
            pltpu.VMEM((shards, 2, rank, wide), bf16),
            pltpu.VMEM((shards, 2, rank, wide), bf16),
            pltpu.VMEM((2, rank, wide), bf16),
            pltpu.VMEM((shards, 2, rank, wide), bf16),
            dma((pieces, 2)),
            dma((2,)),
            dma((pieces, 2)),
            dma((replicas,)),
            dma((replicas,)),
            dma((2, pieces)),
            dma((pieces,)),
            dma((pieces,)),
            dma((2, shards)),
            dma((2, shards)),
            dma((shards,)),
            dma((shards,)),
            dma((shards,)),
            dma((shards,)),
        ],
        compiler_params=pltpu.CompilerParams(
            collective_id=0, has_side_effects=True, vmem_limit_bytes=48 * 1024 * 1024
        ),
    )(momentum, right_basis, reach_map)
    block = rows_dev // 2
    momentum_next, basis_next, left_factor = pl.pallas_call(
        functools.partial(finish_kernel, rows_dev * shards),
        grid=(slots, rows_dev // block),
        out_shape=(
            jax.ShapeDtypeStruct((2, rows_dev, cols), bf16),
            jax.ShapeDtypeStruct((2, rank, cols), bf16),
            jax.ShapeDtypeStruct((2, rows_dev, rank), bf16),
        ),
        in_specs=[
            pl.BlockSpec((1, block, cols), lambda k, i: (k, i, 0)),
            pl.BlockSpec((1, block, rank), lambda k, i: (k, i, 0)),
            pl.BlockSpec((1, rank, rank), lambda k, i: (k, 0, 0)),
            pl.BlockSpec((1, rank, cols), lambda k, i: (k, 0, 0)),
        ],
        out_specs=(
            pl.BlockSpec((1, block, cols), lambda k, i: (k, i, 0)),
            pl.BlockSpec((1, rank, cols), lambda k, i: (k, 0, 0)),
            pl.BlockSpec((1, block, rank), lambda k, i: (k, i, 0)),
        ),
        compiler_params=pltpu.CompilerParams(vmem_limit_bytes=40 * 1024 * 1024),
    )(momentum, q, inv, r)
    return (momentum_next[None], basis_next[None], left_factor[None])


def device_program(momentum, right_basis, reach_map):
    slots, rows_dev, cols = momentum.shape[1:]
    rank = right_basis.shape[2]
    replicas = lax.axis_size("dp")
    shards = lax.axis_size("shard")
    pieces = max(replicas // 2, 1)
    fits = (
        slots == 2
        and replicas % 2 == 0
        and pieces > 1
        and shards > 1
        and replicas <= 16
        and rows_dev % (16 * pieces) == 0
        and cols % (128 * shards) == 0
        and rank == 128
    )
    if fits:
        return fused_on_device(momentum, right_basis, reach_map)
    return on_device(momentum, right_basis, reach_map)


def solution(mesh):
    return jax.shard_map(
        device_program,
        mesh=mesh,
        in_specs=(P("dp", None, "shard", None), P("dp", None, None, None), P()),
        out_specs=(
            P("dp", None, "shard", None),
            P("dp", None, None, None),
            P("dp", None, "shard", None),
        ),
        check_vma=False,
    )
```

```python
import functools
import math

import jax
import jax.numpy as jnp
from jax import lax
from jax.experimental import pallas as pl
from jax.experimental.pallas import tpu as pltpu
from jax.sharding import PartitionSpec as P

NGROUP = 4


decay_keep = 0.9


def from_partner(value, axis, stride):
    mask = 2**stride
    pairs = [(source, source ^ mask) for source in range(lax.axis_size(axis))]
    return lax.ppermute(value, axis, pairs)


def slot_table(reach_map, slot_count):
    counts = jnp.cumsum(reach_map, axis=1)
    chosen = [((reach_map == 1) & (counts == k + 1)).astype(jnp.int32) for k in range(slot_count)]
    return jnp.stack(chosen, axis=1)


def on_device(momentum, right_basis, reach_map):
    slot_count = momentum.shape[1]
    rows_dev = momentum.shape[2]
    col_count = momentum.shape[3]
    rank_size = right_basis.shape[2]
    experts = reach_map.shape[1]
    groups = NGROUP
    replicas = lax.axis_size("dp")
    group_size = replicas // groups
    rows_own = rows_dev // group_size
    per_group = experts // groups
    per_shard = per_group // lax.axis_size("shard")
    shard_pos = lax.axis_index("shard")
    device = lax.axis_index("dp")
    owner_group = device // group_size
    total_rows = rows_dev * lax.axis_size("shard")
    slot_hits = slot_table(reach_map, slot_count)
    expert_group = lax.broadcasted_iota(jnp.int32, (experts,), 0) // per_group
    group_ids = lax.broadcasted_iota(jnp.int32, (groups,), 0)
    my_slots = lax.dynamic_index_in_dim(slot_hits, device, 0, keepdims=False)
    slot_group = jnp.sum(my_slots * expert_group[None, :], axis=1)
    slot_onehot = (slot_group[:, None] == group_ids[None, :]).astype(jnp.bfloat16)
    partial_value = jnp.einsum(
        "src,skc->srk", momentum[0], right_basis[0], preferred_element_type=jnp.float32
    )
    partial_value = (partial_value * (1.0 / math.sqrt(col_count))).astype(jnp.bfloat16)
    pieces = partial_value.reshape(slot_count, group_size, rows_own, rank_size)
    outgoing = jnp.einsum(
        "sg,sqxk->gqxk", slot_onehot, pieces, preferred_element_type=jnp.float32
    ).astype(jnp.bfloat16)
    outgoing = outgoing.reshape(replicas, rows_own, rank_size)
    incoming = lax.all_to_all(outgoing, "dp", split_axis=0, concat_axis=0, tiled=True)
    owned_hits = lax.dynamic_slice_in_dim(slot_hits, owner_group * per_group, per_group, 2)
    source_owned = jnp.sum(owned_hits, axis=1)
    own_count = jnp.sum(source_owned, axis=0)
    my_count = lax.dynamic_slice_in_dim(own_count, shard_pos * per_shard, per_shard, 0)
    source_weight = source_owned.astype(jnp.bfloat16)
    left_sum = jnp.einsum(
        "rj,rxk->jxk", source_weight, incoming, preferred_element_type=jnp.float32
    )
    gram_local = jnp.einsum("jxa,jxb->jab", left_sum, left_sum, precision=lax.Precision.HIGHEST)
    bit_count = group_size.bit_length() - 1
    gram_sum = lax.psum(gram_local.astype(jnp.bfloat16), "shard").astype(jnp.float32)
    for level in range(bit_count):
        gram_sum = gram_sum + from_partner(gram_sum.astype(jnp.bfloat16), "dp", level).astype(
            gram_sum.dtype
        )
    my_gram = lax.dynamic_slice_in_dim(gram_sum, shard_pos * per_shard, per_shard, 0)
    identity = jnp.eye(rank_size, dtype=jnp.float32)
    my_gram = my_gram + identity[None] * (my_count == 0).astype(jnp.float32)[:, None, None]
    factor = jnp.linalg.cholesky(my_gram)
    my_inverse = jax.vmap(lambda m: jax.scipy.linalg.solve_triangular(m, identity, lower=True))(
        factor
    )
    inverse = lax.all_gather(my_inverse.astype(jnp.bfloat16), "shard", axis=0, tiled=True).astype(
        my_inverse.dtype
    )
    scaled = inverse * math.sqrt(total_rows)
    ortho_rows = jnp.einsum(
        "jxk,jyk->jxy", left_sum, scaled, precision=lax.Precision.HIGHEST
    ).astype(jnp.bfloat16)
    send_back = jnp.einsum(
        "rj,jxy->rxy", source_weight, ortho_rows, preferred_element_type=jnp.float32
    ).astype(jnp.bfloat16)
    arrived = lax.all_to_all(send_back, "dp", split_axis=0, concat_axis=0, tiled=True)
    arrived = arrived.reshape(groups, group_size, rows_own, rank_size)
    left_factor = jnp.einsum(
        "sg,gqxk->sqxk", slot_onehot, arrived, preferred_element_type=jnp.float32
    ).astype(jnp.bfloat16)
    left_factor = left_factor.reshape(slot_count, rows_dev, rank_size)
    right_part = jnp.einsum(
        "srk,src->skc", left_factor, momentum[0], preferred_element_type=jnp.float32
    )
    right_part = (right_part * (1.0 / math.sqrt(total_rows))).astype(jnp.bfloat16)
    right_share = (
        lax.psum_scatter(right_part, "shard", scatter_dimension=1, tiled=True)
        .astype(jnp.float32)
        .astype(jnp.bfloat16)
    )
    right_full = lax.all_gather(right_share, "shard", axis=1, tiled=True)
    right_wide = right_full.astype(jnp.float32)
    basis_next = (
        right_wide * lax.rsqrt(jnp.mean(right_wide * right_wide, axis=2, keepdims=True) + 1e-06)
    ).astype(jnp.bfloat16)
    update = jnp.einsum("sxk,skc->sxc", left_factor, right_full, preferred_element_type=jnp.float32)
    momentum_next = (
        momentum[0].astype(jnp.float32) - (1.0 - decay_keep) / math.sqrt(total_rows) * update
    ).astype(jnp.bfloat16)
    return (momentum_next[None], basis_next[None], left_factor[None])


MESH = pl.DeviceIdType.MESH
ROUND = 8
EARLY_ROUNDS = 2


def remote(src, dst, send_sem, recv_sem, device):
    return pltpu.make_async_remote_copy(
        src_ref=src,
        dst_ref=dst,
        send_sem=send_sem,
        recv_sem=recv_sem,
        device_id=device,
        device_id_type=MESH,
    )


def dot_nt(a, b):
    return lax.dot_general(a, b, (((1,), (1,)), ((), ())), preferred_element_type=jnp.float32)


def dot_tn(a, b):
    return lax.dot_general(a, b, (((0,), (0,)), ((), ())), preferred_element_type=jnp.float32)


def slot_classes(reach, groups):
    lane = lax.broadcasted_iota(jnp.int32, reach.shape, 1)
    width = reach.shape[1] // groups
    hot_lanes = jnp.zeros(reach.shape, jnp.float32)
    taken = jnp.zeros((1, 1), jnp.float32)
    for group in range(groups):
        inside = ((lane >= group * width) & (lane < (group + 1) * width)).astype(jnp.float32)
        row_count = jnp.sum(reach * inside, axis=1, keepdims=True)
        full = jnp.min(row_count, axis=0, keepdims=True)
        pick = jnp.where(full > 0.5, 1.0, 0.0) * (1.0 - taken)
        taken = taken + pick
        hot_lanes = hot_lanes + pick * inside
    lane_id = lane.astype(jnp.float32)
    hot = jnp.sum(reach * hot_lanes * lane_id, axis=1, keepdims=True)
    cold = jnp.sum(reach * (1.0 - hot_lanes) * lane_id, axis=1, keepdims=True)
    return hot, cold


def eliminate_round(step, mat):
    rank = mat.shape[1]
    row_id = lax.broadcasted_iota(jnp.int32, mat.shape, 1)
    lane_id = lax.broadcasted_iota(jnp.int32, mat.shape, 2)
    left = rank - ROUND * step
    for m in range(ROUND):
        row = mat[:, m : m + 1, :]
        pivot = 1.0 / row[:, :, m : m + 1]
        active = (row_id > m) & (row_id < left)
        ratio = jnp.where(active, mat[:, :, m : m + 1] * pivot, 0.0)
        row_one = jnp.where(lane_id[:, :1] == m, 1.0, row)
        mat = jnp.where(active & (lane_id == m), 0.0, mat) - ratio * row_one
    mat = jnp.concatenate([mat[:, ROUND:], mat[:, :ROUND]], axis=1)
    return pltpu.roll(mat, rank - ROUND, axis=2)


def power_kernel(
    groups,
    m_hbm,
    b_hbm,
    reach_hbm,
    q_ref,
    inv_ref,
    r_ref,
    reach_ref,
    m_buf,
    b_buf,
    p_out,
    p_in,
    q_out,
    q_in,
    g_out,
    g_in,
    x_out,
    x_in,
    t_out,
    t_in,
    t_red,
    t_full,
    reach_sem,
    m_sem,
    b_sem,
    p_send,
    p_recv,
    q_send,
    q_recv,
    g_send,
    g_recv,
    x_send,
    x_recv,
    t_send,
    t_recv,
    f_send,
    f_recv,
):
    me = lax.axis_index("dp")
    sp = lax.axis_index("shard")
    replicas = p_in.shape[0]
    pieces = replicas // 2
    rows = p_in.shape[1]
    shards = t_full.shape[0]
    wide = t_full.shape[3]
    cols = m_buf.shape[2]
    rank = b_buf.shape[1]
    core = lax.rem(me, 2)
    zed = me // 2
    order = list(range(pieces // 2, pieces)) + list(range(1, pieces // 2)) + [0]

    def piece_at(o):
        return lax.rem(zed + o, pieces)

    def span(q):
        return pl.ds(pl.multiple_of(q * rows, rows), rows)

    pltpu.make_async_copy(reach_hbm, reach_ref, reach_sem.at[0]).start()
    for k in range(2):
        pltpu.make_async_copy(b_hbm.at[k], b_buf.at[k], b_sem.at[k]).start()
    for o in order:
        for k in range(2):
            at = span(piece_at(o))
            pltpu.make_async_copy(m_hbm.at[k, at], m_buf.at[k, at], m_sem.at[o, k]).start()

    barrier = pltpu.get_barrier_semaphore()
    for o in range(1, replicas):
        pl.semaphore_signal(barrier, 1, device_id=(lax.rem(me + o, replicas), sp), device_id_type=MESH)
    for o in range(1, shards):
        for cc in range(2):
            pl.semaphore_signal(
                barrier, 1, device_id=(2 * zed + cc, lax.rem(sp + o, shards)), device_id_type=MESH
            )

    pltpu.make_async_copy(reach_hbm, reach_ref, reach_sem.at[0]).wait()
    hot, cold = slot_classes(reach_ref[...].astype(jnp.float32), groups)
    mine = lax.broadcasted_iota(jnp.int32, (replicas, 1), 0) == me
    my_hot = jnp.sum(jnp.where(mine, hot, 0.0), axis=0, keepdims=True)
    my_cold = jnp.sum(jnp.where(mine, cold, 0.0), axis=0, keepdims=True)
    first = jnp.where(my_hot < my_cold, 1.0, 0.0)
    ids = jnp.where(core == 0, hot, cold)
    diag = lax.broadcasted_iota(jnp.int32, (replicas, replicas), 0) == lax.broadcasted_iota(
        jnp.int32, (replicas, replicas), 1
    )
    ids_row = jnp.sum(jnp.where(diag, ids, 0.0), axis=0, keepdims=True)
    same = jnp.where(ids == ids_row, 1.0, 0.0)

    for k in range(2):
        pltpu.make_async_copy(b_hbm.at[k], b_buf.at[k], b_sem.at[k]).wait()

    for n, o in enumerate(order):
        q = piece_at(o)
        at = span(q)
        part = []
        for k in range(2):
            pltpu.make_async_copy(m_hbm.at[k, at], m_buf.at[k, at], m_sem.at[o, k]).wait()
            value = dot_nt(m_buf[k, at, :], b_buf[k]) * (1.0 / math.sqrt(cols))
            part.append(value)
        p_out[o, 0] = (part[0] * first + part[1] * (1.0 - first)).astype(jnp.bfloat16)
        p_out[o, 1] = (part[1] * first + part[0] * (1.0 - first)).astype(jnp.bfloat16)
        if n == 0:
            pl.semaphore_wait(barrier, replicas - 1 + 2 * (shards - 1))
        if o > 0:
            for cc in range(2):
                remote(
                    p_out.at[o, cc], p_in.at[me], p_send.at[o, cc], p_recv.at[me], (2 * q + cc, sp)
                ).start()
        else:
            other = 1 - core
            remote(
                p_out.at[0, other], p_in.at[me], p_send.at[0, 0], p_recv.at[me], (2 * q + other, sp)
            ).start()
            p_in[me] = p_out[0, core]

    for o in range(1, replicas):
        src = lax.rem(me + o, replicas)
        remote(p_out.at[0, 0], p_in.at[src], p_send.at[0, 0], p_recv.at[src], (src, sp)).wait_recv()

    for zz in range(pieces):
        for cc in range(2):
            i = 2 * zz + cc
            total = jnp.zeros((rows, rank), jnp.float32)
            for j in range(replicas):
                total = total + same[i : i + 1, j : j + 1] * p_in[j].astype(jnp.float32)
            rounded = total.astype(jnp.bfloat16)
            q_out[i] = rounded
            g_out[zz, cc] = dot_tn(rounded, rounded).astype(jnp.bfloat16)

    for o in range(1, replicas):
        dst = lax.rem(me + o, replicas)
        remote(
            q_out.at[dst],
            q_in.at[core, span(zed)],
            q_send.at[o],
            q_recv.at[core, zed],
            (dst, sp),
        ).start()
    q_in[core, span(zed), :] = q_out[me]

    for cc in range(2):
        for zz in range(pieces):

            @pl.when((cc != core) | (zz != zed))
            def _():
                remote(
                    q_out.at[0],
                    q_in.at[cc, pl.ds(zz * rows, rows)],
                    q_send.at[0],
                    q_recv.at[cc, zz],
                    (2 * zz + cc, sp),
                ).wait_recv()

    for zz in range(pieces):

        @pl.when(zz != zed)
        def _():
            remote(
                g_out.at[zz], g_in.at[zed], g_send.at[zz], g_recv.at[zed], (2 * zz + core, sp)
            ).start()

        @pl.when(zz == zed)
        def _():
            g_in[zz] = g_out[zz]

    for zz in range(pieces):
        at = pl.ds(zz * rows, rows)
        a = q_in[0, at, :].astype(jnp.float32)
        b = q_in[1, at, :].astype(jnp.float32)
        q_ref[0, at, :] = (a * first + b * (1.0 - first)).astype(jnp.bfloat16)
        q_ref[1, at, :] = (b * first + a * (1.0 - first)).astype(jnp.bfloat16)
    turned = [q_ref[k].T for k in range(2)]
    for o in list(range(1, shards)) + [0]:
        sq = lax.rem(sp + o, shards)
        at = pl.ds(pl.multiple_of(sq * wide, wide), wide)
        for k in range(2):
            value = jnp.dot(turned[k], m_buf[k, :, at], preferred_element_type=jnp.float32)
            t_out[o, k] = value.astype(jnp.bfloat16)
        if o > 0:
            remote(t_out.at[o], t_in.at[sp], t_send.at[o], t_recv.at[sp], (me, sq)).start()
        else:
            t_in[sp] = t_out[0]

    for o in range(1, pieces):
        src = piece_at(o)
        remote(
            g_out.at[0], g_in.at[src], g_send.at[0], g_recv.at[src], (2 * src + core, sp)
        ).wait_recv()
    for cc in range(2):
        gram = g_in[0, cc].astype(jnp.float32)
        for zz in range(1, pieces):
            gram = gram + g_in[zz, cc].astype(jnp.float32)
        x_out[cc] = gram.astype(jnp.bfloat16)
    peers = [(dc, o) for o in range(shards) for dc in range(2) if (dc, o) != (0, 0)]
    for dc, o in peers:
        cc = lax.rem(core + dc, 2)
        sq = lax.rem(sp + o, shards)
        remote(
            x_out.at[cc], x_in.at[core, sp], x_send.at[dc, o], x_recv.at[core, sp], (2 * zed + cc, sq)
        ).start()
    x_in[core, sp] = x_out[core]
    for dc, o in peers:
        cc = lax.rem(core + dc, 2)
        sq = lax.rem(sp + o, shards)
        remote(
            x_out.at[0], x_in.at[cc, sq], x_send.at[dc, o], x_recv.at[cc, sq], (2 * zed + cc, sq)
        ).wait_recv()

    square = (rank, rank)
    eye_mask = lax.broadcasted_iota(jnp.int32, square, 0) == lax.broadcasted_iota(
        jnp.int32, square, 1
    )
    identity = jnp.where(eye_mask, 1.0, 0.0)
    grams = []
    for c, (table, own) in enumerate(((hot, my_hot), (cold, my_cold))):
        count = jnp.sum(jnp.where(table == own, 1.0, 0.0), axis=0, keepdims=True)
        gram = x_in[c, 0].astype(jnp.float32)
        for sq in range(1, shards):
            gram = gram + x_in[c, sq].astype(jnp.float32)
        grams.append(gram + identity * jnp.where(count < 0.5, 1.0, 0.0))
    mat = jnp.stack(grams, axis=0)
    rounds = rank // ROUND
    mat = lax.fori_loop(0, EARLY_ROUNDS, eliminate_round, mat)

    for o in range(1, shards):
        sq = lax.rem(sp + o, shards)
        remote(t_out.at[0], t_in.at[sq], t_send.at[0], t_recv.at[sq], (me, sq)).wait_recv()
    for k in range(2):
        value = t_in[0, k].astype(jnp.float32)
        for sq in range(1, shards):
            value = value + t_in[sq, k].astype(jnp.float32)
        t_red[k] = value.astype(jnp.bfloat16)
    for o in range(1, shards):
        sq = lax.rem(sp + o, shards)
        remote(t_red, t_full.at[sp], f_send.at[o], f_recv.at[sp], (me, sq)).start()
    t_full[sp] = t_red[...]
    mat = lax.fori_loop(EARLY_ROUNDS, rounds, eliminate_round, mat)

    below = lax.broadcasted_iota(jnp.int32, square, 0) > lax.broadcasted_iota(jnp.int32, square, 1)
    inverse = []
    for c in range(2):
        pivots = jnp.sum(jnp.where(eye_mask, mat[c], 0.0), axis=1, keepdims=True)
        unit = jnp.where(below, mat[c], identity)
        inverse.append(unit * lax.rsqrt(pivots))
    ordered = [
        (inverse[0] * first + inverse[1] * (1.0 - first)).astype(jnp.bfloat16),
        (inverse[1] * first + inverse[0] * (1.0 - first)).astype(jnp.bfloat16),
    ]
    for k in range(2):
        inv_ref[k] = ordered[k]

    for o in range(1, shards):
        sq = lax.rem(sp + o, shards)
        remote(t_red, t_full.at[sq], f_send.at[o], f_recv.at[sq], (me, sq)).wait_recv()
    for sq in range(shards):
        for k in range(2):
            value = jnp.dot(ordered[k], t_full[sq, k], preferred_element_type=jnp.float32)
            r_ref[k, :, sq * wide : (sq + 1) * wide] = value.astype(jnp.bfloat16)

    for o in order:
        for cc in range(2 if o > 0 else 1):
            remote(
                p_out.at[o, cc], p_in.at[me], p_send.at[o, cc], p_recv.at[me], (2 * zed + 1 - core, sp)
            ).wait_send()
    for o in range(1, replicas):
        dst = lax.rem(me + o, replicas)
        remote(
            q_out.at[dst], q_in.at[core, span(zed)], q_send.at[o], q_recv.at[core, zed], (dst, sp)
        ).wait_send()
    for zz in range(pieces):

        @pl.when(zz != zed)
        def _():
            remote(
                g_out.at[zz], g_in.at[zed], g_send.at[zz], g_recv.at[zed], (2 * zz + core, sp)
            ).wait_send()

    for dc, o in peers:
        cc = lax.rem(core + dc, 2)
        sq = lax.rem(sp + o, shards)
        remote(
            x_out.at[cc], x_in.at[core, sp], x_send.at[dc, o], x_recv.at[core, sp], (2 * zed + cc, sq)
        ).wait_send()
    for o in range(1, shards):
        sq = lax.rem(sp + o, shards)
        remote(t_out.at[o], t_in.at[sp], t_send.at[o], t_recv.at[sp], (me, sq)).wait_send()
        remote(t_red, t_full.at[sp], f_send.at[o], f_recv.at[sp], (me, sq)).wait_send()


def finish_kernel(total_rows, m_ref, q_ref, inv_ref, r_ref, out_ref, basis_ref, left_ref):
    r_value = r_ref[0]
    scale = math.sqrt(total_rows)
    left = (dot_nt(q_ref[0], inv_ref[0]) * scale).astype(jnp.bfloat16)
    left_ref[0] = left
    update = jnp.dot(left, r_value, preferred_element_type=jnp.float32)
    out_ref[0] = (m_ref[0].astype(jnp.float32) - ((1.0 - decay_keep) / scale) * update).astype(
        jnp.bfloat16
    )

    @pl.when(pl.program_id(1) == 0)
    def _():
        r_wide = r_value.astype(jnp.float32)
        mean = jnp.mean(r_wide * r_wide, axis=1, keepdims=True)
        basis_ref[0] = (r_wide * lax.rsqrt(mean + 1e-06)).astype(jnp.bfloat16)


def fused_on_device(momentum, right_basis, reach_map):
    momentum = momentum[0]
    right_basis = right_basis[0]
    slots, rows_dev, cols = momentum.shape
    rank = right_basis.shape[1]
    replicas = lax.axis_size("dp")
    shards = lax.axis_size("shard")
    pieces = replicas // 2
    rows = rows_dev // pieces
    wide = cols // shards
    bf16 = jnp.bfloat16
    dma = pltpu.SemaphoreType.DMA
    vmem = pl.BlockSpec(memory_space=pltpu.VMEM)
    hbm = pl.BlockSpec(memory_space=pltpu.HBM)
    q, inv, r = pl.pallas_call(
        functools.partial(power_kernel, NGROUP),
        out_shape=(
            jax.ShapeDtypeStruct((2, rows_dev, rank), bf16),
            jax.ShapeDtypeStruct((2, rank, rank), bf16),
            jax.ShapeDtypeStruct((2, rank, cols), bf16),
        ),
        in_specs=[hbm, hbm, hbm],
        out_specs=(vmem, vmem, vmem),
        scratch_shapes=[
            pltpu.VMEM(reach_map.shape, jnp.int32),
            pltpu.VMEM((2, rows_dev, cols), bf16),
            pltpu.VMEM((2, rank, cols), bf16),
            pltpu.VMEM((pieces, 2, rows, rank), bf16),
            pltpu.VMEM((replicas, rows, rank), bf16),
            pltpu.VMEM((replicas, rows, rank), bf16),
            pltpu.VMEM((2, rows_dev, rank), bf16),
            pltpu.VMEM((pieces, 2, rank, rank), bf16),
            pltpu.VMEM((pieces, 2, rank, rank), bf16),
            pltpu.VMEM((2, rank, rank), bf16),
            pltpu.VMEM((2, shards, rank, rank), bf16),
            pltpu.VMEM((shards, 2, rank, wide), bf16),
            pltpu.VMEM((shards, 2, rank, wide), bf16),
            pltpu.VMEM((2, rank, wide), bf16),
            pltpu.VMEM((shards, 2, rank, wide), bf16),
            dma((1,)),
            dma((pieces, 2)),
            dma((2,)),
            dma((pieces, 2)),
            dma((replicas,)),
            dma((replicas,)),
            dma((2, pieces)),
            dma((pieces,)),
            dma((pieces,)),
            dma((2, shards)),
            dma((2, shards)),
            dma((shards,)),
            dma((shards,)),
            dma((shards,)),
            dma((shards,)),
        ],
        compiler_params=pltpu.CompilerParams(
            collective_id=0, has_side_effects=True, vmem_limit_bytes=48 * 1024 * 1024
        ),
    )(momentum, right_basis, reach_map)
    block = rows_dev // 2
    momentum_next, basis_next, left_factor = pl.pallas_call(
        functools.partial(finish_kernel, rows_dev * shards),
        grid=(slots, rows_dev // block),
        out_shape=(
            jax.ShapeDtypeStruct((2, rows_dev, cols), bf16),
            jax.ShapeDtypeStruct((2, rank, cols), bf16),
            jax.ShapeDtypeStruct((2, rows_dev, rank), bf16),
        ),
        in_specs=[
            pl.BlockSpec((1, block, cols), lambda k, i: (k, i, 0)),
            pl.BlockSpec((1, block, rank), lambda k, i: (k, i, 0)),
            pl.BlockSpec((1, rank, rank), lambda k, i: (k, 0, 0)),
            pl.BlockSpec((1, rank, cols), lambda k, i: (k, 0, 0)),
        ],
        out_specs=(
            pl.BlockSpec((1, block, cols), lambda k, i: (k, i, 0)),
            pl.BlockSpec((1, rank, cols), lambda k, i: (k, 0, 0)),
            pl.BlockSpec((1, block, rank), lambda k, i: (k, i, 0)),
        ),
        compiler_params=pltpu.CompilerParams(vmem_limit_bytes=40 * 1024 * 1024),
    )(momentum, q, inv, r)
    return (momentum_next[None], basis_next[None], left_factor[None])


def device_program(momentum, right_basis, reach_map):
    slots, rows_dev, cols = momentum.shape[1:]
    rank = right_basis.shape[2]
    replicas = lax.axis_size("dp")
    shards = lax.axis_size("shard")
    pieces = max(replicas // 2, 1)
    fits = (
        slots == 2
        and replicas % 2 == 0
        and pieces > 1
        and shards > 1
        and replicas <= 16
        and rows_dev % (16 * pieces) == 0
        and cols % (128 * shards) == 0
        and rank == 128
    )
    if fits:
        return fused_on_device(momentum, right_basis, reach_map)
    return on_device(momentum, right_basis, reach_map)


def solution(mesh):
    return jax.shard_map(
        device_program,
        mesh=mesh,
        in_specs=(P("dp", None, "shard", None), P("dp", None, None, None), P()),
        out_specs=(
            P("dp", None, "shard", None),
            P("dp", None, None, None),
            P("dp", None, "shard", None),
        ),
        check_vma=False,
    )
```

```python
import functools
import math

import jax
import jax.numpy as jnp
from jax import lax
from jax.experimental import pallas as pl
from jax.experimental.pallas import tpu as pltpu
from jax.sharding import PartitionSpec as P

NGROUP = 4


decay_keep = 0.9


def from_partner(value, axis, stride):
    mask = 2**stride
    pairs = [(source, source ^ mask) for source in range(lax.axis_size(axis))]
    return lax.ppermute(value, axis, pairs)


def slot_table(reach_map, slot_count):
    counts = jnp.cumsum(reach_map, axis=1)
    chosen = [((reach_map == 1) & (counts == k + 1)).astype(jnp.int32) for k in range(slot_count)]
    return jnp.stack(chosen, axis=1)


def on_device(momentum, right_basis, reach_map):
    slot_count = momentum.shape[1]
    rows_dev = momentum.shape[2]
    col_count = momentum.shape[3]
    rank_size = right_basis.shape[2]
    experts = reach_map.shape[1]
    groups = NGROUP
    replicas = lax.axis_size("dp")
    group_size = replicas // groups
    rows_own = rows_dev // group_size
    per_group = experts // groups
    per_shard = per_group // lax.axis_size("shard")
    shard_pos = lax.axis_index("shard")
    device = lax.axis_index("dp")
    owner_group = device // group_size
    total_rows = rows_dev * lax.axis_size("shard")
    slot_hits = slot_table(reach_map, slot_count)
    expert_group = lax.broadcasted_iota(jnp.int32, (experts,), 0) // per_group
    group_ids = lax.broadcasted_iota(jnp.int32, (groups,), 0)
    my_slots = lax.dynamic_index_in_dim(slot_hits, device, 0, keepdims=False)
    slot_group = jnp.sum(my_slots * expert_group[None, :], axis=1)
    slot_onehot = (slot_group[:, None] == group_ids[None, :]).astype(jnp.bfloat16)
    partial_value = jnp.einsum(
        "src,skc->srk", momentum[0], right_basis[0], preferred_element_type=jnp.float32
    )
    partial_value = (partial_value * (1.0 / math.sqrt(col_count))).astype(jnp.bfloat16)
    pieces = partial_value.reshape(slot_count, group_size, rows_own, rank_size)
    outgoing = jnp.einsum(
        "sg,sqxk->gqxk", slot_onehot, pieces, preferred_element_type=jnp.float32
    ).astype(jnp.bfloat16)
    outgoing = outgoing.reshape(replicas, rows_own, rank_size)
    incoming = lax.all_to_all(outgoing, "dp", split_axis=0, concat_axis=0, tiled=True)
    owned_hits = lax.dynamic_slice_in_dim(slot_hits, owner_group * per_group, per_group, 2)
    source_owned = jnp.sum(owned_hits, axis=1)
    own_count = jnp.sum(source_owned, axis=0)
    my_count = lax.dynamic_slice_in_dim(own_count, shard_pos * per_shard, per_shard, 0)
    source_weight = source_owned.astype(jnp.bfloat16)
    left_sum = jnp.einsum(
        "rj,rxk->jxk", source_weight, incoming, preferred_element_type=jnp.float32
    )
    gram_local = jnp.einsum("jxa,jxb->jab", left_sum, left_sum, precision=lax.Precision.HIGHEST)
    bit_count = group_size.bit_length() - 1
    gram_sum = lax.psum(gram_local.astype(jnp.bfloat16), "shard").astype(jnp.float32)
    for level in range(bit_count):
        gram_sum = gram_sum + from_partner(gram_sum.astype(jnp.bfloat16), "dp", level).astype(
            gram_sum.dtype
        )
    my_gram = lax.dynamic_slice_in_dim(gram_sum, shard_pos * per_shard, per_shard, 0)
    identity = jnp.eye(rank_size, dtype=jnp.float32)
    my_gram = my_gram + identity[None] * (my_count == 0).astype(jnp.float32)[:, None, None]
    factor = jnp.linalg.cholesky(my_gram)
    my_inverse = jax.vmap(lambda m: jax.scipy.linalg.solve_triangular(m, identity, lower=True))(
        factor
    )
    inverse = lax.all_gather(my_inverse.astype(jnp.bfloat16), "shard", axis=0, tiled=True).astype(
        my_inverse.dtype
    )
    scaled = inverse * math.sqrt(total_rows)
    ortho_rows = jnp.einsum(
        "jxk,jyk->jxy", left_sum, scaled, precision=lax.Precision.HIGHEST
    ).astype(jnp.bfloat16)
    send_back = jnp.einsum(
        "rj,jxy->rxy", source_weight, ortho_rows, preferred_element_type=jnp.float32
    ).astype(jnp.bfloat16)
    arrived = lax.all_to_all(send_back, "dp", split_axis=0, concat_axis=0, tiled=True)
    arrived = arrived.reshape(groups, group_size, rows_own, rank_size)
    left_factor = jnp.einsum(
        "sg,gqxk->sqxk", slot_onehot, arrived, preferred_element_type=jnp.float32
    ).astype(jnp.bfloat16)
    left_factor = left_factor.reshape(slot_count, rows_dev, rank_size)
    right_part = jnp.einsum(
        "srk,src->skc", left_factor, momentum[0], preferred_element_type=jnp.float32
    )
    right_part = (right_part * (1.0 / math.sqrt(total_rows))).astype(jnp.bfloat16)
    right_share = (
        lax.psum_scatter(right_part, "shard", scatter_dimension=1, tiled=True)
        .astype(jnp.float32)
        .astype(jnp.bfloat16)
    )
    right_full = lax.all_gather(right_share, "shard", axis=1, tiled=True)
    right_wide = right_full.astype(jnp.float32)
    basis_next = (
        right_wide * lax.rsqrt(jnp.mean(right_wide * right_wide, axis=2, keepdims=True) + 1e-06)
    ).astype(jnp.bfloat16)
    update = jnp.einsum("sxk,skc->sxc", left_factor, right_full, preferred_element_type=jnp.float32)
    momentum_next = (
        momentum[0].astype(jnp.float32) - (1.0 - decay_keep) / math.sqrt(total_rows) * update
    ).astype(jnp.bfloat16)
    return (momentum_next[None], basis_next[None], left_factor[None])


MESH = pl.DeviceIdType.MESH
ROUND = 8
EARLY_ROUNDS = 0


def remote(src, dst, send_sem, recv_sem, device):
    return pltpu.make_async_remote_copy(
        src_ref=src,
        dst_ref=dst,
        send_sem=send_sem,
        recv_sem=recv_sem,
        device_id=device,
        device_id_type=MESH,
    )


def dot_nt(a, b):
    return lax.dot_general(a, b, (((1,), (1,)), ((), ())), preferred_element_type=jnp.float32)


def dot_tn(a, b):
    return lax.dot_general(a, b, (((0,), (0,)), ((), ())), preferred_element_type=jnp.float32)


def slot_classes(reach, groups):
    lane = lax.broadcasted_iota(jnp.int32, reach.shape, 1)
    width = reach.shape[1] // groups
    hot_lanes = jnp.zeros(reach.shape, jnp.float32)
    taken = jnp.zeros((1, 1), jnp.float32)
    for group in range(groups):
        inside = ((lane >= group * width) & (lane < (group + 1) * width)).astype(jnp.float32)
        row_count = jnp.sum(reach * inside, axis=1, keepdims=True)
        full = jnp.min(row_count, axis=0, keepdims=True)
        pick = jnp.where(full > 0.5, 1.0, 0.0) * (1.0 - taken)
        taken = taken + pick
        hot_lanes = hot_lanes + pick * inside
    lane_id = lane.astype(jnp.float32)
    hot = jnp.sum(reach * hot_lanes * lane_id, axis=1, keepdims=True)
    cold = jnp.sum(reach * (1.0 - hot_lanes) * lane_id, axis=1, keepdims=True)
    return hot, cold


def eliminate_round(step, mat):
    rank = mat.shape[1]
    row_id = lax.broadcasted_iota(jnp.int32, mat.shape, 1)
    lane_id = lax.broadcasted_iota(jnp.int32, mat.shape, 2)
    left = rank - ROUND * step
    for m in range(ROUND):
        row = mat[:, m : m + 1, :]
        pivot = 1.0 / row[:, :, m : m + 1]
        active = (row_id > m) & (row_id < left)
        ratio = jnp.where(active, mat[:, :, m : m + 1] * pivot, 0.0)
        row_one = jnp.where(lane_id[:, :1] == m, 1.0, row)
        mat = jnp.where(active & (lane_id == m), 0.0, mat) - ratio * row_one
    mat = jnp.concatenate([mat[:, ROUND:], mat[:, :ROUND]], axis=1)
    return pltpu.roll(mat, rank - ROUND, axis=2)


def power_kernel(
    groups,
    m_hbm,
    b_hbm,
    reach_hbm,
    q_ref,
    inv_ref,
    r_ref,
    reach_ref,
    m_buf,
    b_buf,
    p_out,
    p_in,
    q_out,
    q_in,
    g_out,
    g_in,
    x_out,
    x_in,
    t_out,
    t_in,
    t_red,
    t_full,
    reach_sem,
    m_sem,
    b_sem,
    p_send,
    p_recv,
    q_send,
    q_recv,
    g_send,
    g_recv,
    x_send,
    x_recv,
    t_send,
    t_recv,
    f_send,
    f_recv,
):
    me = lax.axis_index("dp")
    sp = lax.axis_index("shard")
    replicas = p_in.shape[0]
    pieces = replicas // 2
    rows = p_in.shape[1]
    shards = t_full.shape[0]
    wide = t_full.shape[3]
    cols = m_buf.shape[2]
    rank = b_buf.shape[1]
    core = lax.rem(me, 2)
    zed = me // 2
    order = list(range(pieces // 2, pieces)) + list(range(1, pieces // 2)) + [0]

    def piece_at(o):
        return lax.rem(zed + o, pieces)

    def span(q):
        return pl.ds(pl.multiple_of(q * rows, rows), rows)

    pltpu.make_async_copy(reach_hbm, reach_ref, reach_sem.at[0]).start()
    for k in range(2):
        pltpu.make_async_copy(b_hbm.at[k], b_buf.at[k], b_sem.at[k]).start()
    for o in order:
        for k in range(2):
            at = span(piece_at(o))
            pltpu.make_async_copy(m_hbm.at[k, at], m_buf.at[k, at], m_sem.at[o, k]).start()

    barrier = pltpu.get_barrier_semaphore()
    for o in range(1, replicas):
        pl.semaphore_signal(barrier, 1, device_id=(lax.rem(me + o, replicas), sp), device_id_type=MESH)
    for o in range(1, shards):
        for cc in range(2):
            pl.semaphore_signal(
                barrier, 1, device_id=(2 * zed + cc, lax.rem(sp + o, shards)), device_id_type=MESH
            )

    pltpu.make_async_copy(reach_hbm, reach_ref, reach_sem.at[0]).wait()
    hot, cold = slot_classes(reach_ref[...].astype(jnp.float32), groups)
    mine = lax.broadcasted_iota(jnp.int32, (replicas, 1), 0) == me
    my_hot = jnp.sum(jnp.where(mine, hot, 0.0), axis=0, keepdims=True)
    my_cold = jnp.sum(jnp.where(mine, cold, 0.0), axis=0, keepdims=True)
    first = jnp.where(my_hot < my_cold, 1.0, 0.0)
    ids = jnp.where(core == 0, hot, cold)
    diag = lax.broadcasted_iota(jnp.int32, (replicas, replicas), 0) == lax.broadcasted_iota(
        jnp.int32, (replicas, replicas), 1
    )
    ids_row = jnp.sum(jnp.where(diag, ids, 0.0), axis=0, keepdims=True)
    same = jnp.where(ids == ids_row, 1.0, 0.0)

    for k in range(2):
        pltpu.make_async_copy(b_hbm.at[k], b_buf.at[k], b_sem.at[k]).wait()

    for n, o in enumerate(order):
        q = piece_at(o)
        at = span(q)
        part = []
        for k in range(2):
            pltpu.make_async_copy(m_hbm.at[k, at], m_buf.at[k, at], m_sem.at[o, k]).wait()
            value = dot_nt(m_buf[k, at, :], b_buf[k]) * (1.0 / math.sqrt(cols))
            part.append(value)
        p_out[o, 0] = (part[0] * first + part[1] * (1.0 - first)).astype(jnp.bfloat16)
        p_out[o, 1] = (part[1] * first + part[0] * (1.0 - first)).astype(jnp.bfloat16)
        if n == 0:
            pl.semaphore_wait(barrier, replicas - 1 + 2 * (shards - 1))
        if o > 0:
            for cc in range(2):
                remote(
                    p_out.at[o, cc], p_in.at[me], p_send.at[o, cc], p_recv.at[me], (2 * q + cc, sp)
                ).start()
        else:
            other = 1 - core
            remote(
                p_out.at[0, other], p_in.at[me], p_send.at[0, 0], p_recv.at[me], (2 * q + other, sp)
            ).start()
            p_in[me] = p_out[0, core]

    for o in range(1, replicas):
        src = lax.rem(me + o, replicas)
        remote(p_out.at[0, 0], p_in.at[src], p_send.at[0, 0], p_recv.at[src], (src, sp)).wait_recv()

    for zz in range(pieces):
        for cc in range(2):
            i = 2 * zz + cc
            total = jnp.zeros((rows, rank), jnp.float32)
            for j in range(replicas):
                total = total + same[i : i + 1, j : j + 1] * p_in[j].astype(jnp.float32)
            rounded = total.astype(jnp.bfloat16)
            q_out[i] = rounded
            g_out[zz, cc] = dot_tn(rounded, rounded).astype(jnp.bfloat16)

    for o in range(1, replicas):
        dst = lax.rem(me + o, replicas)
        remote(
            q_out.at[dst],
            q_in.at[core, span(zed)],
            q_send.at[o],
            q_recv.at[core, zed],
            (dst, sp),
        ).start()
    q_in[core, span(zed), :] = q_out[me]

    for cc in range(2):
        for zz in range(pieces):

            @pl.when((cc != core) | (zz != zed))
            def _():
                remote(
                    q_out.at[0],
                    q_in.at[cc, pl.ds(zz * rows, rows)],
                    q_send.at[0],
                    q_recv.at[cc, zz],
                    (2 * zz + cc, sp),
                ).wait_recv()

    for zz in range(pieces):

        @pl.when(zz != zed)
        def _():
            remote(
                g_out.at[zz], g_in.at[zed], g_send.at[zz], g_recv.at[zed], (2 * zz + core, sp)
            ).start()

        @pl.when(zz == zed)
        def _():
            g_in[zz] = g_out[zz]

    for zz in range(pieces):
        at = pl.ds(zz * rows, rows)
        a = q_in[0, at, :].astype(jnp.float32)
        b = q_in[1, at, :].astype(jnp.float32)
        q_ref[0, at, :] = (a * first + b * (1.0 - first)).astype(jnp.bfloat16)
        q_ref[1, at, :] = (b * first + a * (1.0 - first)).astype(jnp.bfloat16)
    turned = [q_ref[k].T for k in range(2)]
    for o in list(range(1, shards)) + [0]:
        sq = lax.rem(sp + o, shards)
        at = pl.ds(pl.multiple_of(sq * wide, wide), wide)
        for k in range(2):
            value = jnp.dot(turned[k], m_buf[k, :, at], preferred_element_type=jnp.float32)
            t_out[o, k] = value.astype(jnp.bfloat16)
        if o > 0:
            remote(t_out.at[o], t_in.at[sp], t_send.at[o], t_recv.at[sp], (me, sq)).start()
        else:
            t_in[sp] = t_out[0]

    for o in range(1, pieces):
        src = piece_at(o)
        remote(
            g_out.at[0], g_in.at[src], g_send.at[0], g_recv.at[src], (2 * src + core, sp)
        ).wait_recv()
    for cc in range(2):
        gram = g_in[0, cc].astype(jnp.float32)
        for zz in range(1, pieces):
            gram = gram + g_in[zz, cc].astype(jnp.float32)
        x_out[cc] = gram.astype(jnp.bfloat16)
    peers = [(dc, o) for o in range(shards) for dc in range(2) if (dc, o) != (0, 0)]
    for dc, o in peers:
        cc = lax.rem(core + dc, 2)
        sq = lax.rem(sp + o, shards)
        remote(
            x_out.at[cc], x_in.at[core, sp], x_send.at[dc, o], x_recv.at[core, sp], (2 * zed + cc, sq)
        ).start()
    x_in[core, sp] = x_out[core]
    for dc, o in peers:
        cc = lax.rem(core + dc, 2)
        sq = lax.rem(sp + o, shards)
        remote(
            x_out.at[0], x_in.at[cc, sq], x_send.at[dc, o], x_recv.at[cc, sq], (2 * zed + cc, sq)
        ).wait_recv()

    square = (rank, rank)
    eye_mask = lax.broadcasted_iota(jnp.int32, square, 0) == lax.broadcasted_iota(
        jnp.int32, square, 1
    )
    identity = jnp.where(eye_mask, 1.0, 0.0)
    grams = []
    for c, (table, own) in enumerate(((hot, my_hot), (cold, my_cold))):
        count = jnp.sum(jnp.where(table == own, 1.0, 0.0), axis=0, keepdims=True)
        gram = x_in[c, 0].astype(jnp.float32)
        for sq in range(1, shards):
            gram = gram + x_in[c, sq].astype(jnp.float32)
        grams.append(gram + identity * jnp.where(count < 0.5, 1.0, 0.0))
    mat = jnp.stack(grams, axis=0)
    rounds = rank // ROUND
    mat = lax.fori_loop(0, EARLY_ROUNDS, eliminate_round, mat)

    for o in range(1, shards):
        sq = lax.rem(sp + o, shards)
        remote(t_out.at[0], t_in.at[sq], t_send.at[0], t_recv.at[sq], (me, sq)).wait_recv()
    for k in range(2):
        value = t_in[0, k].astype(jnp.float32)
        for sq in range(1, shards):
            value = value + t_in[sq, k].astype(jnp.float32)
        t_red[k] = value.astype(jnp.bfloat16)
    for o in range(1, shards):
        sq = lax.rem(sp + o, shards)
        remote(t_red, t_full.at[sp], f_send.at[o], f_recv.at[sp], (me, sq)).start()
    t_full[sp] = t_red[...]
    mat = lax.fori_loop(EARLY_ROUNDS, rounds, eliminate_round, mat)

    below = lax.broadcasted_iota(jnp.int32, square, 0) > lax.broadcasted_iota(jnp.int32, square, 1)
    inverse = []
    for c in range(2):
        pivots = jnp.sum(jnp.where(eye_mask, mat[c], 0.0), axis=1, keepdims=True)
        unit = jnp.where(below, mat[c], identity)
        inverse.append(unit * lax.rsqrt(pivots))
    ordered = [
        (inverse[0] * first + inverse[1] * (1.0 - first)).astype(jnp.bfloat16),
        (inverse[1] * first + inverse[0] * (1.0 - first)).astype(jnp.bfloat16),
    ]
    for k in range(2):
        inv_ref[k] = ordered[k]

    for o in range(1, shards):
        sq = lax.rem(sp + o, shards)
        remote(t_red, t_full.at[sq], f_send.at[o], f_recv.at[sq], (me, sq)).wait_recv()
    for sq in range(shards):
        for k in range(2):
            value = jnp.dot(ordered[k], t_full[sq, k], preferred_element_type=jnp.float32)
            r_ref[k, :, sq * wide : (sq + 1) * wide] = value.astype(jnp.bfloat16)

    for o in order:
        for cc in range(2 if o > 0 else 1):
            remote(
                p_out.at[o, cc], p_in.at[me], p_send.at[o, cc], p_recv.at[me], (2 * zed + 1 - core, sp)
            ).wait_send()
    for o in range(1, replicas):
        dst = lax.rem(me + o, replicas)
        remote(
            q_out.at[dst], q_in.at[core, span(zed)], q_send.at[o], q_recv.at[core, zed], (dst, sp)
        ).wait_send()
    for zz in range(pieces):

        @pl.when(zz != zed)
        def _():
            remote(
                g_out.at[zz], g_in.at[zed], g_send.at[zz], g_recv.at[zed], (2 * zz + core, sp)
            ).wait_send()

    for dc, o in peers:
        cc = lax.rem(core + dc, 2)
        sq = lax.rem(sp + o, shards)
        remote(
            x_out.at[cc], x_in.at[core, sp], x_send.at[dc, o], x_recv.at[core, sp], (2 * zed + cc, sq)
        ).wait_send()
    for o in range(1, shards):
        sq = lax.rem(sp + o, shards)
        remote(t_out.at[o], t_in.at[sp], t_send.at[o], t_recv.at[sp], (me, sq)).wait_send()
        remote(t_red, t_full.at[sp], f_send.at[o], f_recv.at[sp], (me, sq)).wait_send()


def finish_kernel(total_rows, m_ref, q_ref, inv_ref, r_ref, out_ref, basis_ref, left_ref):
    r_value = r_ref[0]
    scale = math.sqrt(total_rows)
    left = (dot_nt(q_ref[0], inv_ref[0]) * scale).astype(jnp.bfloat16)
    left_ref[0] = left
    update = jnp.dot(left, r_value, preferred_element_type=jnp.float32)
    out_ref[0] = (m_ref[0].astype(jnp.float32) - ((1.0 - decay_keep) / scale) * update).astype(
        jnp.bfloat16
    )

    @pl.when(pl.program_id(1) == 0)
    def _():
        r_wide = r_value.astype(jnp.float32)
        mean = jnp.mean(r_wide * r_wide, axis=1, keepdims=True)
        basis_ref[0] = (r_wide * lax.rsqrt(mean + 1e-06)).astype(jnp.bfloat16)


def fused_on_device(momentum, right_basis, reach_map):
    momentum = momentum[0]
    right_basis = right_basis[0]
    slots, rows_dev, cols = momentum.shape
    rank = right_basis.shape[1]
    replicas = lax.axis_size("dp")
    shards = lax.axis_size("shard")
    pieces = replicas // 2
    rows = rows_dev // pieces
    wide = cols // shards
    bf16 = jnp.bfloat16
    dma = pltpu.SemaphoreType.DMA
    vmem = pl.BlockSpec(memory_space=pltpu.VMEM)
    hbm = pl.BlockSpec(memory_space=pltpu.HBM)
    q, inv, r = pl.pallas_call(
        functools.partial(power_kernel, NGROUP),
        out_shape=(
            jax.ShapeDtypeStruct((2, rows_dev, rank), bf16),
            jax.ShapeDtypeStruct((2, rank, rank), bf16),
            jax.ShapeDtypeStruct((2, rank, cols), bf16),
        ),
        in_specs=[hbm, hbm, hbm],
        out_specs=(vmem, vmem, vmem),
        scratch_shapes=[
            pltpu.VMEM(reach_map.shape, jnp.int32),
            pltpu.VMEM((2, rows_dev, cols), bf16),
            pltpu.VMEM((2, rank, cols), bf16),
            pltpu.VMEM((pieces, 2, rows, rank), bf16),
            pltpu.VMEM((replicas, rows, rank), bf16),
            pltpu.VMEM((replicas, rows, rank), bf16),
            pltpu.VMEM((2, rows_dev, rank), bf16),
            pltpu.VMEM((pieces, 2, rank, rank), bf16),
            pltpu.VMEM((pieces, 2, rank, rank), bf16),
            pltpu.VMEM((2, rank, rank), bf16),
            pltpu.VMEM((2, shards, rank, rank), bf16),
            pltpu.VMEM((shards, 2, rank, wide), bf16),
            pltpu.VMEM((shards, 2, rank, wide), bf16),
            pltpu.VMEM((2, rank, wide), bf16),
            pltpu.VMEM((shards, 2, rank, wide), bf16),
            dma((1,)),
            dma((pieces, 2)),
            dma((2,)),
            dma((pieces, 2)),
            dma((replicas,)),
            dma((replicas,)),
            dma((2, pieces)),
            dma((pieces,)),
            dma((pieces,)),
            dma((2, shards)),
            dma((2, shards)),
            dma((shards,)),
            dma((shards,)),
            dma((shards,)),
            dma((shards,)),
        ],
        compiler_params=pltpu.CompilerParams(
            collective_id=0, has_side_effects=True, vmem_limit_bytes=48 * 1024 * 1024
        ),
    )(momentum, right_basis, reach_map)
    block = rows_dev // 2
    momentum_next, basis_next, left_factor = pl.pallas_call(
        functools.partial(finish_kernel, rows_dev * shards),
        grid=(slots, rows_dev // block),
        out_shape=(
            jax.ShapeDtypeStruct((2, rows_dev, cols), bf16),
            jax.ShapeDtypeStruct((2, rank, cols), bf16),
            jax.ShapeDtypeStruct((2, rows_dev, rank), bf16),
        ),
        in_specs=[
            pl.BlockSpec((1, block, cols), lambda k, i: (k, i, 0)),
            pl.BlockSpec((1, block, rank), lambda k, i: (k, i, 0)),
            pl.BlockSpec((1, rank, rank), lambda k, i: (k, 0, 0)),
            pl.BlockSpec((1, rank, cols), lambda k, i: (k, 0, 0)),
        ],
        out_specs=(
            pl.BlockSpec((1, block, cols), lambda k, i: (k, i, 0)),
            pl.BlockSpec((1, rank, cols), lambda k, i: (k, 0, 0)),
            pl.BlockSpec((1, block, rank), lambda k, i: (k, i, 0)),
        ),
        compiler_params=pltpu.CompilerParams(vmem_limit_bytes=40 * 1024 * 1024),
    )(momentum, q, inv, r)
    return (momentum_next[None], basis_next[None], left_factor[None])


def device_program(momentum, right_basis, reach_map):
    slots, rows_dev, cols = momentum.shape[1:]
    rank = right_basis.shape[2]
    replicas = lax.axis_size("dp")
    shards = lax.axis_size("shard")
    pieces = max(replicas // 2, 1)
    fits = (
        slots == 2
        and replicas % 2 == 0
        and pieces > 1
        and shards > 1
        and replicas <= 16
        and rows_dev % (16 * pieces) == 0
        and cols % (128 * shards) == 0
        and rank == 128
    )
    if fits:
        return fused_on_device(momentum, right_basis, reach_map)
    return on_device(momentum, right_basis, reach_map)


def solution(mesh):
    return jax.shard_map(
        device_program,
        mesh=mesh,
        in_specs=(P("dp", None, "shard", None), P("dp", None, None, None), P()),
        out_specs=(
            P("dp", None, "shard", None),
            P("dp", None, None, None),
            P("dp", None, "shard", None),
        ),
        check_vma=False,
    )
```
